256 devices in a mesh: pipe: 16 (over z_lo, x, core), tp: 16 (over y, z_hi).
Axes of the slice: x: 4, y: 4, z: 8 (z_hi: 4, z_lo: 2; z = z_hi * 2 + z_lo), core: 2. Of those that a mesh axis runs over, the one named last changes fastest.
Arguments:
- x_fwd: bfloat16 [16, 256, 6144], P('pipe', None, 'tp'), may hold values from -6 to 6
- cotangent: bfloat16 [16, 256, 6144], P('pipe', None, 'tp'), may hold values from -6 to 6
- ln_gain: bfloat16 [16, 6144], P('pipe', 'tp'), may hold values from 0.5 to 2
- ln_bias: bfloat16 [16, 6144], P('pipe', 'tp'), may hold values from -3 to 3
- w_value: bfloat16 [16, 6144, 6144], P('pipe', None, 'tp'), may hold values from -1 to 1
- w_out: bfloat16 [16, 6144, 6144], P('pipe', 'tp'), may hold values from -0.15625 to 0.15625
- scores_fwd: float32 [16, 48, 256, 256], P('pipe', 'tp'), may hold values from -9 to 400, as said below
- scores_bwd: float32 [16, 48, 256, 256], P('pipe', 'tp'), may hold values from -9 to 400, as said below
- stash_codes: bfloat16 [16, 256, 6144], P('pipe', None, 'tp'), may hold values from -448 to 448
- stash_scales: bfloat16 [16, 48, 256], P('pipe', 'tp'), may hold values from 0.005 to 0.151
- evict: int32 [16, 256], P('pipe'), may hold values from 0 to 15, as said below
Outputs:
- fwd_next: bfloat16 [16, 256, 6144], P('pipe', None, 'tp')
- bwd_next: bfloat16 [16, 256, 6144], P('pipe', None, 'tp')
The draws below stay inside these ranges and needn't reach their ends.
Inputs may be any that keep to these rules, and one draw needn't show every extreme that they name: `scores_fwd`: pre-softmax scores. `scores_bwd`: pre-softmax scores. evict[s, t] is s or 15 - s, and evict[evict[s, t], t] = s; every token of section 0 has its stash held by section 15.
All inputs are finite; a program needn't handle non-finite values.
Results may differ from the reference program's by a relative error of at most 0.017.
Values may be sent and summed in bfloat16 or wider, within the bound.
No kernel may reach another device: no remote copies, remote signals or barrier semaphores. Data moves between devices by JAX's collectives and lax.ppermute only.
A program may use at most 64 MiB of HBM per device.

```python
import math
import jax
import jax.numpy as jnp
from jax import lax

D = 6144
HEADS = 48
HD = 128
QB = 128
ROWS = 256
HV = 6144
SECTIONS = 16
N_TP = 16


def pair_direction(key):
    base = jnp.clip(jax.random.normal(jax.random.fold_in(key, 31), (SECTIONS, D), jnp.float32), -3.0, 3.0)
    section_index = lax.broadcasted_iota(jnp.int32, (SECTIONS, D), 0)
    return jnp.where(section_index < SECTIONS - 1 - section_index, base, base[::-1])


def draw_w_value(key, part):
    direction = pair_direction(key)
    key = jax.random.fold_in(key, 13)
    key_noise, key_right = jax.random.split(key, 2)
    noise = jnp.clip(jax.random.normal(key_noise, (SECTIONS, D, HV), jnp.float32), -6.0, 6.0)
    right = jnp.clip(jax.random.normal(key_right, (SECTIONS, HV), jnp.float32), -3.0, 3.0)
    return ((noise + 2.0 * direction[:, :, None] * right[:, None, :]) / math.sqrt(5.0 * D)).astype(jnp.bfloat16)


def draw_stash_codes(key, part):
    direction = pair_direction(key)
    key = jax.random.fold_in(key, 17)
    key_noise, key_sign, key_strength, key_offset = jax.random.split(key, 4)
    shape = (SECTIONS, ROWS, D)
    sign = jnp.where(jax.random.bernoulli(key_sign, 0.5, (SECTIONS, ROWS, 1)), 1.0, -1.0)
    noise = 24.0 * jnp.clip(jax.random.normal(key_noise, shape, jnp.float32), -6.0, 6.0)
    strength = jax.random.uniform(key_strength, (SECTIONS, ROWS, 1), jnp.float32, 0.6, 1.4)
    offset = jax.random.uniform(key_offset, (SECTIONS, ROWS, 1), jnp.float32, -48.0, 48.0)
    codes = noise + 48.0 * sign * strength * direction[:, None, :] + offset
    return jnp.clip(codes, -448.0, 448.0).astype(jnp.bfloat16)


def draw_scores_fwd(key, part):
    key = jax.random.fold_in(key, 11)
    key_base = jax.random.fold_in(key, 0)
    shape = (SECTIONS, HEADS, ROWS, ROWS)
    return jnp.clip(jax.random.normal(key_base, shape, jnp.float32), -6.0, 6.0) * 1.5


def draw_scores_bwd(key, part):
    key = jax.random.fold_in(key, 23)
    key_base = jax.random.fold_in(key, 0)
    shape = (SECTIONS, HEADS, ROWS, ROWS)
    return jnp.clip(jax.random.normal(key_base, shape, jnp.float32), -6.0, 6.0) * 1.5


def draw_stash_scales(key, part):
    key = jax.random.fold_in(key, 7)
    key_cell = jax.random.fold_in(key, 0)
    block_total = D // QB
    shape = (SECTIONS, block_total, ROWS)
    block_index = lax.broadcasted_iota(jnp.float32, shape, 1)
    rising = jnp.exp(math.log(3.0) * block_index / max(block_total - 1, 1))
    cell_scale = jnp.exp(jax.random.uniform(key_cell, shape, jnp.float32, math.log(0.005), math.log(0.05)))
    return jnp.clip(cell_scale * rising, 0.005, 0.15).astype(jnp.bfloat16)


def draw_evict(key, part):
    key = jax.random.fold_in(key, 5)
    coin = jax.random.randint(key, (SECTIONS, ROWS), 0, 2)
    section_index = lax.broadcasted_iota(jnp.int32, (SECTIONS, ROWS), 0)
    mirror_index = SECTIONS - 1 - section_index
    pair_index = jnp.minimum(section_index, mirror_index)
    pair_coin = jnp.take(coin, pair_index[:, 0], axis=0)
    moved = (pair_coin == 1) | (pair_index == 0)
    return jnp.where(moved, mirror_index, section_index).astype(jnp.int32)


def block_levels(own_key, dims, shards, least, top_value):
    factor_of = 1.0
    for dim, parts in shards:
        steps = jax.random.uniform(jax.random.fold_in(jax.random.fold_in(own_key, 6), dim), (parts,), jnp.float32, least / len(shards), top_value / len(shards))
        factor_of = factor_of * jnp.repeat(jnp.exp(steps), dims[dim] // parts).reshape((-1,) + (1,) * (len(dims) - 1 - dim))
    return factor_of


def bell_draw(key, extent, scale, most, cuts=(), dtype=jnp.bfloat16):
    values = scale * jax.random.normal(key, extent, jnp.float32)
    if cuts:
        values = values * block_levels(key, extent, cuts, -0.22, 0.18)
    return jnp.clip(values, -most, most).astype(dtype)


def setup_inputs(seed: int = 0) -> dict:
    key_of = jax.random.split(jax.random.key(seed), 12)
    x_fwd = bell_draw(key_of[0], (SECTIONS, ROWS, D), 1.0, 6.0, ((0, 16), (2, 16)))
    cotangent = bell_draw(key_of[1], (SECTIONS, ROWS, D), 1.0, 6.0, ((0, 16), (2, 16)))
    ln_gain = jnp.clip(jnp.exp(math.log(2.0) - 1.3862944 * jax.random.uniform(key_of[2], (SECTIONS, D), jnp.float32) ** block_levels(key_of[2], (SECTIONS, D), ((0, 16), (1, 16)), -0.2, 0.2)), 0.5, 2.0).astype(jnp.bfloat16)
    ln_bias = bell_draw(key_of[3], (SECTIONS, D), 0.5, 3.0, ((0, 16), (1, 16)))
    w_value = draw_w_value(jax.random.fold_in(key_of[11], 71), 0)
    w_out = bell_draw(key_of[5], (SECTIONS, HV, D), (HV // 4) ** -0.5, 0.15625, ((0, 16), (1, 16)))
    scores_fwd = draw_scores_fwd(jax.random.fold_in(key_of[11], 71), 0)
    scores_bwd = draw_scores_bwd(jax.random.fold_in(key_of[11], 71), 0)
    stash_codes = draw_stash_codes(jax.random.fold_in(key_of[11], 71), 0)
    stash_scales = draw_stash_scales(jax.random.fold_in(key_of[11], 71), 0)
    evict = draw_evict(jax.random.fold_in(key_of[11], 71), 0)
    return {"x_fwd": x_fwd, "cotangent": cotangent, "ln_gain": ln_gain, "ln_bias": ln_bias, "w_value": w_value, "w_out": w_out, "scores_fwd": scores_fwd, "scores_bwd": scores_bwd, "stash_codes": stash_codes, "stash_scales": stash_scales, "evict": evict}


norm_epsilon = 1e-05

def causal_weights(scores):
    query_pos = lax.broadcasted_iota(jnp.int32, scores.shape, scores.ndim - 2)
    key_pos = lax.broadcasted_iota(jnp.int32, scores.shape, scores.ndim - 1)
    masked = jnp.where(key_pos <= query_pos, scores, -jnp.inf)
    highest = lax.optimization_barrier(jnp.max(masked, axis=-1, keepdims=True))
    raised = jnp.exp(masked - highest)
    return (raised / lax.optimization_barrier(jnp.sum(raised, axis=-1, keepdims=True))).astype(jnp.bfloat16)

def group_sum(left, right, transposed):
    group_width = left.shape[1] // N_TP
    if transposed:
        total = jnp.zeros((left.shape[0], right.shape[0]), jnp.float32)
    else:
        total = jnp.zeros((left.shape[0], right.shape[1]), jnp.float32)
    for group_index in range(N_TP):
        left_part = left[:, group_index * group_width:(group_index + 1) * group_width]
        if transposed:
            right_part = right[:, group_index * group_width:(group_index + 1) * group_width].T
        else:
            right_part = right[group_index * group_width:(group_index + 1) * group_width, :]
        partial_term = jnp.dot(left_part, right_part, preferred_element_type=jnp.float32).astype(jnp.bfloat16)
        partial_term = lax.optimization_barrier(partial_term)
        total = total + partial_term.astype(jnp.float32)
    return total

def one_section(pieces):
    tokens, upstream, gain_row, bias_row, value_proj, out_proj, score_fwd, score_bwd, held_codes, held_scales = pieces
    tokens_wide = tokens.astype(jnp.float32)
    row_mean = lax.optimization_barrier(jnp.sum(tokens_wide, axis=-1, keepdims=True)) / D
    row_var = lax.optimization_barrier(jnp.sum(tokens_wide * tokens_wide, axis=-1, keepdims=True)) / D - row_mean * row_mean
    normed = ((tokens_wide - row_mean) * lax.rsqrt(row_var + norm_epsilon) * gain_row.astype(jnp.float32) + bias_row.astype(jnp.float32)).astype(jnp.bfloat16)
    values = jnp.dot(normed, value_proj, preferred_element_type=jnp.float32).astype(jnp.bfloat16)
    weights_fwd = causal_weights(score_fwd)
    mixed = jnp.einsum('hqk,khd->qhd', weights_fwd.astype(jnp.float32), values.reshape(ROWS, HEADS, HD).astype(jnp.float32))
    mixed = mixed.astype(jnp.bfloat16).reshape(ROWS, HV)
    section_out = (tokens_wide + group_sum(mixed, out_proj, False)).astype(jnp.bfloat16)
    grad_mixed = jnp.dot(upstream, out_proj.T, preferred_element_type=jnp.float32).astype(jnp.bfloat16)
    weights_bwd = causal_weights(score_bwd)
    grad_values = jnp.einsum('hqk,qhd->khd', weights_bwd.astype(jnp.float32), grad_mixed.reshape(ROWS, HEADS, HD).astype(jnp.float32))
    grad_values = grad_values.astype(jnp.bfloat16).reshape(ROWS, HV)
    grad_normed = group_sum(grad_values, value_proj, True)
    stashed = (held_codes.astype(jnp.float32).reshape(ROWS, D // QB, QB) * held_scales.astype(jnp.float32).T[:, :, None]).reshape(ROWS, D)
    stash_mean = lax.optimization_barrier(jnp.sum(stashed, axis=-1, keepdims=True)) / D
    stash_var = lax.optimization_barrier(jnp.sum(stashed * stashed, axis=-1, keepdims=True)) / D - stash_mean * stash_mean
    inv_std = lax.rsqrt(stash_var + norm_epsilon)
    grad_scaled = grad_normed * gain_row.astype(jnp.float32)
    grad_mean = lax.optimization_barrier(jnp.sum(grad_scaled, axis=-1, keepdims=True)) / D
    cross_mean = lax.optimization_barrier(jnp.sum(grad_scaled * stashed, axis=-1, keepdims=True)) / D
    centred = (stashed - stash_mean) * inv_std
    grad_input = inv_std * (grad_scaled - grad_mean - centred * inv_std * (cross_mean - stash_mean * grad_mean))
    grad_input = (upstream.astype(jnp.float32) + grad_input).astype(jnp.bfloat16)
    return (section_out, grad_input)

def reference(x_fwd, cotangent, ln_gain, ln_bias, w_value, w_out, scores_fwd, scores_bwd, stash_codes, stash_scales, evict):
    section_index = lax.broadcasted_iota(jnp.int32, evict.shape, 0)
    keep_own = evict == section_index
    held_codes = jnp.where(keep_own[:, :, None], stash_codes, stash_codes[::-1])
    held_scales = jnp.where(keep_own[:, None, :], stash_scales, stash_scales[::-1])
    section_out, grad_input = lax.map(one_section, (x_fwd, cotangent, ln_gain, ln_bias, w_value, w_out, scores_fwd, scores_bwd, held_codes, held_scales))
    fwd_next = jnp.concatenate([jnp.zeros_like(section_out[:1]), section_out[:-1]], axis=0)
    bwd_next = jnp.concatenate([grad_input[1:], jnp.zeros_like(grad_input[:1])], axis=0)
    return (fwd_next, bwd_next)
```

```python
import jax
import jax.numpy as jnp
from jax import lax
from jax.experimental import pallas as pl
from jax.experimental.pallas import tpu as pltpu
from jax.sharding import Mesh, PartitionSpec as P

norm_epsilon = 1e-05
SIDE = 4
F32 = jnp.float32
BF16 = jnp.bfloat16
NT = (((1,), (1,)), ((), ()))
NN = (((1,), (0,)), ((), ()))
VMEM_LIMIT = 40 * 1024 * 1024


def turned(value, axis, steps):
    return lax.ppermute(value, axis, [(i, (i + steps) % SIDE) for i in range(SIDE)])


def shifted(value, axis, steps):
    count = lax.axis_size(axis)
    first, last = (max(0, -steps), min(count, count - steps))
    return lax.ppermute(value, axis, [(source, source + steps) for source in range(first, last)])


def shifted_turned(value, steps):
    count = lax.axis_size("pipe")
    pairs = [
        (s * SIDE + i, (s + 1) * SIDE + (i + steps) % SIDE)
        for s in range(count - 1)
        for i in range(SIDE)
    ]
    return lax.ppermute(value, ("pipe", "z"), pairs)


def mirrored(value):
    count = lax.axis_size("pipe")
    return lax.ppermute(value, "pipe", [(s, count - 1 - s) for s in range(count)])


def after(value, *others):
    return lax.optimization_barrier((value, *others))[0]


def add(left, right):
    return (left.astype(F32) + right.astype(F32)).astype(BF16)


def weights_kernel(fwd_ref, bwd_ref, fwd_out, bwd_out):
    size = fwd_ref.shape[-1]
    query = lax.broadcasted_iota(jnp.int32, (size, size), 0)
    key = lax.broadcasted_iota(jnp.int32, (size, size), 1)

    def causal(scores):
        masked = jnp.where(key <= query, scores, -jnp.inf)
        raised = jnp.exp(masked - jnp.max(masked, axis=-1, keepdims=True))
        return raised / jnp.sum(raised, axis=-1, keepdims=True)

    for head in range(fwd_ref.shape[0]):
        bwd_out[head] = causal(bwd_ref[head]).T.astype(BF16)
        fwd_out[head] = causal(fwd_ref[head]).astype(BF16)


def start_weights(place, wv_hbm, wo_hbm, wv, wo, sem_v, sem_o, value_first, order):
    width = wv_hbm.shape[1]

    def copies(j):
        block = lax.rem(place[0] + j // SIDE, SIDE) * SIDE + lax.rem(place[1] + j % SIDE, SIDE)
        at = pl.ds(pl.multiple_of(block * width, 128), width)
        here = slice(j * width, (j + 1) * width)
        return (
            pltpu.make_async_copy(wv_hbm.at[at, :], wv.at[here, :], sem_v.at[j]),
            pltpu.make_async_copy(wo_hbm.at[:, at], wo.at[:, here], sem_o.at[j]),
        )

    both = [copies(j) for j in range(SIDE * SIDE)]
    value, out = [b[0] for b in both], [b[1] for b in both]
    first, second = (value, out) if value_first else (out, value)
    for c in first:
        c.start()
    for pair in order:
        second[2 * pair].start()
        second[2 * pair + 1].start()
    return value, out


def bwd_kernel(
    place, g, l, r, fa, fb, wbt, wv_hbm, wo_hbm,
    p2a, p2b, p1b, p3a, p1a, p3b, p0, wv, wo, sem_v, sem_o,
):
    width = g.shape[2]
    outs = [(p0, 0), (p0, 2), (p1a, 0), (p1b, 0), (p2a, 0), (p2b, 0), (p3a, 0), (p3b, 0)]
    order = [4, 5, 3, 6, 2, 7, 0, 1]
    value, out = start_weights(place, wv_hbm, wo_hbm, wv, wo, sem_v, sem_o, False, order)
    pieces = [(g, 0), (g, 2), (r, 0), (r, 2), (fa, 0), (fb, 0), (l, 0), (l, 2)]
    total = jnp.zeros(g.shape[1:], F32)
    for pair, (ref, at) in enumerate(pieces):
        out[2 * pair].wait()
        out[2 * pair + 1].wait()
        wide = jnp.concatenate([ref[at], ref[at + 1]], axis=1)
        total += lax.dot_general(
            wide, wo[:, 2 * pair * width : 2 * (pair + 1) * width], NT, preferred_element_type=F32
        )
    mixed = total.astype(BF16)
    size = width // wbt.shape[0]
    grads = [
        lax.dot_general(
            wbt[h], mixed[:, h * size : (h + 1) * size], NN, preferred_element_type=F32
        ).astype(BF16)
        for h in range(wbt.shape[0])
    ]
    grads = jnp.concatenate(grads, axis=1)
    for pair in order:
        value[2 * pair].wait()
        value[2 * pair + 1].wait()
        ref, at = outs[pair]
        wide = lax.dot_general(
            grads, wv[2 * pair * width : 2 * (pair + 1) * width, :], NT, preferred_element_type=F32
        ).astype(BF16)
        ref[at] = wide[:, :width]
        ref[at + 1] = wide[:, width:]


def fwd_kernel(
    place, g, l, r, fa, fb, wf, wv_hbm, wo_hbm,
    p2a, p2b, p1b, p3a, p1a, p3b, p0, wv, wo, sem_v, sem_o,
):
    rows, width = p0.shape[1:]
    outs = [(p0, 0), (p0, 2), (p1a, 0), (p1b, 0), (p2a, 0), (p2b, 0), (p3a, 0), (p3b, 0)]
    order = [4, 5, 3, 6, 2, 7, 0, 1]
    value, out = start_weights(place, wv_hbm, wo_hbm, wv, wo, sem_v, sem_o, True, order)
    pieces = [(g, 0), (g, 2), (r, 0), (r, 2), (fa, 0), (fb, 0), (l, 0), (l, 2)]
    full = width * SIDE * SIDE
    sums = jnp.zeros((rows, 128), F32)
    squares = jnp.zeros((rows, 128), F32)
    for ref, at in pieces:
        for one in (at, at + 1):
            for c in range(0, width, 128):
                part = ref[one, :rows, c : c + 128].astype(F32)
                sums += part
                squares += part * part
    mean = jnp.sum(sums, axis=-1, keepdims=True) / full
    var = jnp.sum(squares, axis=-1, keepdims=True) / full - mean * mean
    inv_std = lax.rsqrt(var + norm_epsilon)
    total = jnp.zeros((rows, width), F32)
    for pair, (ref, at) in enumerate(pieces):
        value[2 * pair].wait()
        value[2 * pair + 1].wait()
        normed = []
        for one in (at, at + 1):
            affine = ref[one, rows : rows + 16, :].astype(F32)
            part = ref[one, :rows, :].astype(F32)
            normed.append(
                ((part - mean) * inv_std * affine[0:1] + affine[1:2]).astype(BF16)
            )
        wide = jnp.concatenate(normed, axis=1)
        total += lax.dot_general(
            wide, wv[2 * pair * width : 2 * (pair + 1) * width, :], NN, preferred_element_type=F32
        )
    values = total.astype(BF16)
    size = width // wf.shape[0]
    mixed = [
        lax.dot_general(
            wf[h], values[:, h * size : (h + 1) * size], NN, preferred_element_type=F32
        ).astype(BF16)
        for h in range(wf.shape[0])
    ]
    mixed = jnp.concatenate(mixed, axis=1)
    for pair in order:
        out[2 * pair].wait()
        out[2 * pair + 1].wait()
        ref, at = outs[pair]
        wide = lax.dot_general(
            mixed, wo[:, 2 * pair * width : 2 * (pair + 1) * width], NN, preferred_element_type=F32
        ).astype(BF16)
        ref[at] = wide[:, :width]
        ref[at + 1] = wide[:, width:]


def project(kernel, place, pieces, weights, w_value, w_out, rows):
    width = w_value.shape[1]
    half = jax.ShapeDtypeStruct((2, rows, width), BF16)
    whole = jax.ShapeDtypeStruct((4, rows, width), BF16)
    vmem = pl.BlockSpec(memory_space=pltpu.VMEM)
    hbm = pl.BlockSpec(memory_space=pl.ANY)
    blocks = SIDE * SIDE
    flops = 4 * rows * width * width * blocks + 4 * rows * rows * width
    moved = 2 * 2 * width * width * blocks + 4 * rows * width * blocks
    return pl.pallas_call(
        kernel,
        out_shape=[half] * 6 + [whole],
        in_specs=[pl.BlockSpec(memory_space=pltpu.SMEM)] + [vmem] * 6 + [hbm] * 2,
        out_specs=[vmem] * 7,
        scratch_shapes=[
            pltpu.VMEM((blocks * width, width), BF16),
            pltpu.VMEM((width, blocks * width), BF16),
            pltpu.SemaphoreType.DMA((blocks,)),
            pltpu.SemaphoreType.DMA((blocks,)),
        ],
        cost_estimate=pl.CostEstimate(flops=flops, bytes_accessed=moved, transcendentals=0),
        compiler_params=pltpu.CompilerParams(vmem_limit_bytes=VMEM_LIMIT),
    )(place, *pieces, weights, w_value, w_out)


def near(value):
    return jnp.stack([value, turned(value, "z", -1), turned(value, "z", 2), turned(value, "z", 1)])


def far(group):
    left, right = turned(group, "y", 1), turned(group, "y", -1)
    return (group, left, right, turned(left[:2], "y", 1), turned(right[2:], "y", -1))


def scatter_far(parts):
    p2a, p2b, p1b, p3a, p1a, p3b, p0 = parts
    to_right, to_left = turned(p2a, "y", 1), turned(p2b, "y", -1)
    right_b, left_a = turned(p1b, "y", 1), turned(p3a, "y", -1)
    right_a = turned(add(p1a, to_right), "y", 1)
    left_b = turned(add(p3b, to_left), "y", -1)

    def three(a, b, c):
        return (a.astype(F32) + b.astype(F32) + c.astype(F32)).astype(BF16)

    first, second = three(p0[:2], right_a, left_a), three(p0[2:], right_b, left_b)
    return first[0], first[1], second[0], second[1]


def summed(value, axis):
    return value + turned(value, axis, 1) + turned(value, axis, 2) + turned(value, axis, -1)


def per_device(
    x_fwd,
    cotangent,
    ln_gain,
    ln_bias,
    w_value,
    w_out,
    scores_fwd,
    scores_bwd,
    stash_codes,
    stash_scales,
    evict,
):
    tokens, upstream = x_fwd[0], cotangent[0]
    rows, width = tokens.shape
    full = width * SIDE * SIDE
    value_proj, out_proj = w_value[0], w_out[0]
    place = jnp.stack([lax.axis_index("y"), lax.axis_index("z")]).astype(jnp.int32)

    group_up = near(upstream)
    affine = jnp.concatenate([ln_gain, ln_bias, jnp.zeros((14, width), BF16)], axis=0)
    tokens_affine = jnp.concatenate([tokens, affine], axis=0)
    tokens_affine = after(tokens_affine, group_up)
    group_tok = near(tokens_affine)
    pieces_up = far(group_up)
    pieces_tok = far(group_tok)

    heads = scores_fwd.shape[1:]
    weights_fwd, weights_bwd = pl.pallas_call(
        weights_kernel,
        out_shape=[jax.ShapeDtypeStruct(heads, BF16)] * 2,
        compiler_params=pltpu.CompilerParams(vmem_limit_bytes=VMEM_LIMIT),
    )(scores_fwd[0], scores_bwd[0])

    codes, scales = after((stash_codes[0], stash_scales[0]), group_tok)
    residual = after(tokens, group_tok)
    far_codes, far_scales = mirrored(codes), mirrored(scales)
    residual = shifted(residual, "pipe", 1)

    parts_bwd = project(bwd_kernel, place, pieces_up, weights_bwd, value_proj, out_proj, rows)
    q0, q1, q2, q3 = scatter_far(parts_bwd)
    r1, r2, r3 = turned(q1, "z", 1), turned(q2, "z", 2), turned(q3, "z", -1)

    parts_fwd = project(fwd_kernel, place, pieces_tok, weights_fwd, value_proj, out_proj, rows)
    f0, f1, f2, f3 = scatter_far(parts_fwd)
    s0, s1 = shifted_turned(f0, 0), shifted_turned(f1, 1)
    s2, s3 = shifted_turned(f2, 2), shifted_turned(f3, -1)

    keep_own = evict[0] == lax.axis_index("pipe")
    held_codes = jnp.where(keep_own[:, None], stash_codes[0], far_codes)
    held_scales = jnp.where(keep_own[None, :], stash_scales[0], far_scales)
    blocks = held_scales.shape[0]
    stashed = (
        held_codes.astype(F32).reshape(rows, blocks, width // blocks)
        * held_scales.astype(F32).T[:, :, None]
    ).reshape(rows, width)

    grad_normed = q0.astype(F32) + r1.astype(F32) + r2.astype(F32) + r3.astype(F32)
    grad_scaled = grad_normed * ln_gain[0].astype(F32)
    sums = jnp.stack(
        [
            jnp.sum(stashed, axis=-1),
            jnp.sum(stashed * stashed, axis=-1),
            jnp.sum(grad_scaled, axis=-1),
            jnp.sum(grad_scaled * stashed, axis=-1),
        ]
    )
    sums = summed(summed(sums, "z"), "y") / full
    stash_mean, square_mean, grad_mean, cross_mean = (sums[i][:, None] for i in range(4))
    inv_std = lax.rsqrt(square_mean - stash_mean * stash_mean + norm_epsilon)
    centred = (stashed - stash_mean) * inv_std
    grad_input = inv_std * (
        grad_scaled - grad_mean - centred * inv_std * (cross_mean - stash_mean * grad_mean)
    )
    grad_input = (upstream.astype(F32) + grad_input).astype(BF16)
    bwd_next = shifted(grad_input, "pipe", -1)

    fwd_next = residual.astype(F32) + s0.astype(F32) + s1.astype(F32) + s2.astype(F32)
    fwd_next = (fwd_next + s3.astype(F32)).astype(BF16)
    return (fwd_next[None], bwd_next[None])


def solution(mesh):
    pipe = mesh.devices.shape[0]
    split = Mesh(mesh.devices.reshape(pipe, SIDE, SIDE), ("pipe", "y", "z"))
    tp = ("y", "z")
    placed = (
        P("pipe", None, tp),
        P("pipe", None, tp),
        P("pipe", tp),
        P("pipe", tp),
        P("pipe", None, tp),
        P("pipe", tp, None),
        P("pipe", tp, None, None),
        P("pipe", tp, None, None),
        P("pipe", None, tp),
        P("pipe", tp, None),
        P("pipe", None),
    )
    return jax.shard_map(
        per_device,
        mesh=split,
        in_specs=placed,
        out_specs=(P("pipe", None, tp), P("pipe", None, tp)),
        check_vma=False,
    )
```

```python
import jax
import jax.numpy as jnp
from jax import lax
from jax.experimental import pallas as pl
from jax.experimental.pallas import tpu as pltpu
from jax.sharding import Mesh, PartitionSpec as P

norm_epsilon = 1e-05
SIDE = 4
F32 = jnp.float32
BF16 = jnp.bfloat16
NT = (((1,), (1,)), ((), ()))
NN = (((1,), (0,)), ((), ()))
VMEM_LIMIT = 56 * 1024 * 1024


def turned(value, axis, steps):
    return lax.ppermute(value, axis, [(i, (i + steps) % SIDE) for i in range(SIDE)])


def shifted(value, axis, steps):
    count = lax.axis_size(axis)
    first, last = (max(0, -steps), min(count, count - steps))
    return lax.ppermute(value, axis, [(source, source + steps) for source in range(first, last)])


def shifted_turned(value, steps):
    count = lax.axis_size("pipe")
    pairs = [
        (s * SIDE + i, (s + 1) * SIDE + (i + steps) % SIDE)
        for s in range(count - 1)
        for i in range(SIDE)
    ]
    return lax.ppermute(value, ("pipe", "z"), pairs)


def mirrored(value):
    count = lax.axis_size("pipe")
    return lax.ppermute(value, "pipe", [(s, count - 1 - s) for s in range(count)])


def add(left, right):
    return (left.astype(F32) + right.astype(F32)).astype(BF16)


def weights_kernel(fwd_ref, bwd_ref, fwd_out, bwd_out):
    size = fwd_ref.shape[-1]
    query = lax.broadcasted_iota(jnp.int32, (size, size), 0)
    key = lax.broadcasted_iota(jnp.int32, (size, size), 1)

    def causal(scores):
        masked = jnp.where(key <= query, scores, -jnp.inf)
        raised = jnp.exp(masked - jnp.max(masked, axis=-1, keepdims=True))
        return raised / jnp.sum(raised, axis=-1, keepdims=True)

    for head in range(fwd_ref.shape[0]):
        bwd_out[head] = causal(bwd_ref[head]).T.astype(BF16)
        fwd_out[head] = causal(fwd_ref[head]).astype(BF16)


ORDER = [4, 5, 3, 6, 2, 7, 0, 1]


def start_weights(place, wv_hbm, wo_hbm, wv, wo, sem_v, sem_o, value_first):
    width = wv_hbm.shape[1]

    def copies(j, second):
        relative = second or (value_first and j // SIDE == 2)
        k = lax.rem(place[1] + j % SIDE, SIDE) if relative else j % SIDE
        block = lax.rem(place[0] + j // SIDE, SIDE) * SIDE + k
        at = pl.ds(pl.multiple_of(block * width, 128), width)
        here = slice(j * width, (j + 1) * width)
        if second != value_first:
            return pltpu.make_async_copy(wv_hbm.at[at, :], wv.at[here, :], sem_v.at[j])
        return pltpu.make_async_copy(wo_hbm.at[:, at], wo.at[:, here], sem_o.at[j])

    first = [copies(j, False) for j in range(SIDE * SIDE)]
    second = [copies(j, True) for j in range(SIDE * SIDE)]
    for c in first:
        c.start()
    for pair in ORDER:
        second[2 * pair].start()
        second[2 * pair + 1].start()
    return first, second


def start_pieces(refs, held, sem):
    near, right, left, far_a, far_b = refs
    two, three = pl.ds(0, 2), pl.ds(0, 3)
    if len(far_a.shape) == 2:
        far = [(far_a, held.at[8]), (far_b.at[three], held.at[pl.ds(9, 3)])]
    else:
        far = [(far_a.at[two], held.at[pl.ds(8, 2)]), (far_b.at[two], held.at[pl.ds(10, 2)])]
    moves = [
        (near, held.at[pl.ds(0, 4)]),
        (right, held.at[pl.ds(4, 4)]),
        *far,
        (left, held.at[pl.ds(12, 4)]),
    ]
    copies = [pltpu.make_async_copy(*move, sem.at[i]) for i, move in enumerate(moves)]
    for c in copies:
        c.start()
    return [copies[0:1], [], copies[1:2], [], copies[2:4], [], copies[4:5], []]


def give_parts(product, refs, parts, sem, width):
    p2a, p2b, p1, p3, p0 = refs
    outs = [(p0, 0), (p0, 2), (p1, 0), (p1, 2), (p2a, 0), (p2b, 0), (p3, 0), (p3, 2)]
    copies = []
    for pair in ORDER:
        ref, at = outs[pair]
        wide = product(pair).astype(BF16)
        parts[2 * pair] = wide[:, :width]
        parts[2 * pair + 1] = wide[:, width:]
        copies.append(
            pltpu.make_async_copy(
                parts.at[pl.ds(2 * pair, 2)], ref.at[pl.ds(at, 2)], sem.at[pair]
            )
        )
        copies[-1].start()
    for c in copies:
        c.wait()


def mix(weights, values):
    size = values.shape[1] // weights.shape[0]
    heads = [
        lax.dot_general(
            weights[h], values[:, h * size : (h + 1) * size], NN, preferred_element_type=F32
        ).astype(BF16)
        for h in range(weights.shape[0])
    ]
    return jnp.concatenate(heads, axis=1)


def bwd_kernel(
    place, near, right, left, fa, fb, weights, wv_hbm, wo_hbm,
    p2a, p2b, p1, p3, p0,
    held, parts, wv, wo, sem_in, sem_out, sem_v, sem_o,
):
    rows, width = parts.shape[1:]
    arriving = start_pieces((near, right, left, fa, fb), held, sem_in)
    out, value = start_weights(place, wv_hbm, wo_hbm, wv, wo, sem_v, sem_o, False)
    total = jnp.zeros((rows, width), F32)
    for pair in range(SIDE * SIDE // 2):
        for c in arriving[pair]:
            c.wait()
        out[2 * pair].wait()
        out[2 * pair + 1].wait()
        wide = jnp.concatenate([held[2 * pair], held[2 * pair + 1]], axis=1)
        total += lax.dot_general(
            wide, wo[:, 2 * pair * width : 2 * (pair + 1) * width], NT, preferred_element_type=F32
        )
    grads = mix(weights, total.astype(BF16))

    def product(pair):
        value[2 * pair].wait()
        value[2 * pair + 1].wait()
        return lax.dot_general(
            grads, wv[2 * pair * width : 2 * (pair + 1) * width, :], NT, preferred_element_type=F32
        )

    give_parts(product, (p2a, p2b, p1, p3, p0), parts, sem_out, width)


def fwd_kernel(
    place, near, right, left, fa, fb, weights, wv_hbm, wo_hbm,
    p2a, p2b, p1, p3, p0,
    held, parts, wv, wo, sem_in, sem_out, sem_v, sem_o,
):
    rows, width = parts.shape[1:]
    arriving = start_pieces((near, right, left, fa, fb), held, sem_in)
    value, out = start_weights(place, wv_hbm, wo_hbm, wv, wo, sem_v, sem_o, True)
    full = width * SIDE * SIDE
    sums = jnp.zeros((rows, 128), F32)
    squares = jnp.zeros((rows, 128), F32)
    for one in range(SIDE * SIDE):
        if one % 2 == 0:
            for c in arriving[one // 2]:
                c.wait()
        for c in range(0, width, 128):
            part = held[one, :rows, c : c + 128].astype(F32)
            sums += part
            squares += part * part
    mean = jnp.sum(sums, axis=-1, keepdims=True) / full
    var = jnp.sum(squares, axis=-1, keepdims=True) / full - mean * mean
    inv_std = lax.rsqrt(var + norm_epsilon)
    total = jnp.zeros((rows, width), F32)
    for pair in range(SIDE * SIDE // 2):
        value[2 * pair].wait()
        value[2 * pair + 1].wait()
        normed = []
        for one in (2 * pair, 2 * pair + 1):
            affine = held[one, rows : rows + 16, :].astype(F32)
            part = held[one, :rows, :].astype(F32)
            normed.append(((part - mean) * inv_std * affine[0:1] + affine[1:2]).astype(BF16))
        wide = jnp.concatenate(normed, axis=1)
        total += lax.dot_general(
            wide, wv[2 * pair * width : 2 * (pair + 1) * width, :], NN, preferred_element_type=F32
        )
    mixed = mix(weights, total.astype(BF16))

    def product(pair):
        out[2 * pair].wait()
        out[2 * pair + 1].wait()
        return lax.dot_general(
            mixed, wo[:, 2 * pair * width : 2 * (pair + 1) * width], NN, preferred_element_type=F32
        )

    give_parts(product, (p2a, p2b, p1, p3, p0), parts, sem_out, width)


def project(kernel, place, pieces, weights, w_value, w_out, rows):
    width = w_value.shape[1]
    half = jax.ShapeDtypeStruct((2, rows, width), BF16)
    whole = jax.ShapeDtypeStruct((4, rows, width), BF16)
    hbm = pl.BlockSpec(memory_space=pl.ANY)
    blocks = SIDE * SIDE
    flops = 4 * rows * width * width * blocks + 4 * rows * rows * width
    moved = 2 * 2 * width * width * blocks + 4 * rows * width * blocks
    return pl.pallas_call(
        kernel,
        out_shape=[half] * 2 + [whole] * 3,
        in_specs=[pl.BlockSpec(memory_space=pltpu.SMEM)]
        + [hbm] * 5
        + [pl.BlockSpec(memory_space=pltpu.VMEM)]
        + [hbm] * 2,
        out_specs=[hbm] * 5,
        scratch_shapes=[
            pltpu.VMEM((blocks, pieces[0].shape[1], width), BF16),
            pltpu.VMEM((blocks, rows, width), BF16),
            pltpu.VMEM((blocks * width, width), BF16),
            pltpu.VMEM((width, blocks * width), BF16),
            pltpu.SemaphoreType.DMA((blocks // 2,)),
            pltpu.SemaphoreType.DMA((blocks // 2,)),
            pltpu.SemaphoreType.DMA((blocks,)),
            pltpu.SemaphoreType.DMA((blocks,)),
        ],
        cost_estimate=pl.CostEstimate(flops=flops, bytes_accessed=moved, transcendentals=0),
        compiler_params=pltpu.CompilerParams(vmem_limit_bytes=VMEM_LIMIT),
    )(place, *pieces, weights, w_value, w_out)


def around(value):
    return turned(value, "z", -1), turned(value, "z", 2), turned(value, "z", 1)


def both_sides(value):
    return turned(value, "y", -1), turned(value, "y", 1)


def relayed(right, left):
    return turned(left[:2], "y", 1), turned(right[2:], "y", -1)


def joined(parts, by_left, by_right):
    _, _, p1, p3, p0 = parts
    p1 = jnp.concatenate([add(p1[:2], by_left), p1[2:]], axis=0)
    p3 = jnp.concatenate([p3[:2], add(p3[2:], by_right)], axis=0)
    return p1, p3, p0


def three(a, b, c):
    return (a.astype(F32) + b.astype(F32) + c.astype(F32)).astype(BF16)


def summed(value, axis):
    return value + turned(value, axis, 2) + turned(value, axis, 1) + turned(value, axis, -1)


def per_device(
    x_fwd,
    cotangent,
    ln_gain,
    ln_bias,
    w_value,
    w_out,
    scores_fwd,
    scores_bwd,
    stash_codes,
    stash_scales,
    evict,
):
    tokens, upstream = x_fwd[0], cotangent[0]
    rows, width = tokens.shape
    full = width * SIDE * SIDE
    value_proj, out_proj = w_value[0], w_out[0]
    place = jnp.stack([lax.axis_index("y"), lax.axis_index("z")]).astype(jnp.int32)

    ordered = lax.optimization_barrier
    affine = jnp.concatenate([ln_gain, ln_bias, jnp.zeros((14, width), BF16)], axis=0)
    tokens_affine = jnp.concatenate([tokens, affine], axis=0)
    near_up = lax.all_gather(upstream, "z", axis=0)
    right_up, left_up = both_sides(near_up)
    across = turned(tokens_affine, "y", 2)
    near_tok = lax.all_gather(tokens_affine, "z", axis=0)
    right_up, left_up, near_tok, across = ordered((right_up, left_up, near_tok, across))
    far_up = relayed(right_up, left_up)
    across_z = around(across)
    heads = scores_fwd.shape[1:]
    weights_fwd, weights_bwd = pl.pallas_call(
        weights_kernel,
        out_shape=[jax.ShapeDtypeStruct(heads, BF16)] * 2,
        compiler_params=pltpu.CompilerParams(vmem_limit_bytes=VMEM_LIMIT),
    )(scores_fwd[0], scores_bwd[0])

    far_up, near_tok, weights_bwd = ordered((far_up, near_tok, weights_bwd))
    right_tok, left_tok = both_sides(near_tok)

    projections = (value_proj, out_proj, rows)
    pieces_up = (near_up, right_up, left_up, *far_up)
    parts_bwd = project(bwd_kernel, place, pieces_up, weights_bwd, *projections)
    codes, scales = stash_codes[0], stash_scales[0]
    parts_bwd, across_z, codes, scales = ordered((parts_bwd, across_z, codes, scales))
    across_z = jnp.stack(across_z)
    blocks = scales.shape[0]
    scale_rows = blocks * rows // width
    fill = jnp.zeros((16 - scale_rows, width), BF16)
    stash = jnp.concatenate([codes, scales.reshape(scale_rows, width), fill])
    far_stash = mirrored(stash)
    passing_bwd = turned(parts_bwd[0], "y", 1), turned(parts_bwd[1], "y", -1)
    right_tok, left_tok, passing_bwd = ordered((right_tok, left_tok, passing_bwd))
    pieces_tok = (near_tok, right_tok, left_tok, across, across_z)
    p1, p3, p0 = joined(parts_bwd, *passing_bwd)
    by_left, by_right = turned(p1, "y", 1), turned(p3, "y", -1)
    parts_fwd = project(fwd_kernel, place, pieces_tok, weights_fwd, *projections)
    by_left, by_right, parts_fwd, far_stash = ordered((by_left, by_right, parts_fwd, far_stash))

    passing_fwd = turned(parts_fwd[0], "y", 1), turned(parts_fwd[1], "y", -1)
    by_left, by_right, passing_fwd = ordered((by_left, by_right, passing_fwd))
    q0, q1, q2, q3 = three(p0, by_left, by_right)
    r2, r1, r3 = turned(q2, "z", 2), turned(q1, "z", 1), turned(q3, "z", -1)
    p1, p3, p0 = joined(parts_fwd, *passing_fwd)
    by_left, by_right = turned(p1, "y", 1), turned(p3, "y", -1)
    by_left, by_right, r1, r2, r3 = ordered((by_left, by_right, r1, r2, r3))
    f0, f1, f2, f3 = three(p0, by_left, by_right)
    f0 = add(f0, tokens)
    s2, s1 = shifted_turned(f2, 2), shifted_turned(f1, 1)
    s3, s0 = shifted_turned(f3, -1), shifted_turned(f0, 0)

    keep_own = evict[0] == lax.axis_index("pipe")
    far_scales = far_stash[rows : rows + scale_rows].reshape(blocks, rows)
    held_codes = jnp.where(keep_own[:, None], codes, far_stash[:rows])
    held_scales = jnp.where(keep_own[None, :], scales, far_scales)
    stashed = (
        held_codes.astype(F32).reshape(rows, blocks, width // blocks)
        * held_scales.astype(F32).T[:, :, None]
    ).reshape(rows, width)

    grad_normed = q0.astype(F32) + r1.astype(F32) + r2.astype(F32) + r3.astype(F32)
    grad_scaled = grad_normed * ln_gain[0].astype(F32)
    sums = jnp.stack(
        [
            jnp.sum(stashed, axis=-1),
            jnp.sum(stashed * stashed, axis=-1),
            jnp.sum(grad_scaled, axis=-1),
            jnp.sum(grad_scaled * stashed, axis=-1),
        ]
    )
    sums, s2 = ordered((summed(sums, "z"), s2))
    sums = summed(sums, "y") / full
    stash_mean, square_mean, grad_mean, cross_mean = (sums[i][:, None] for i in range(4))
    inv_std = lax.rsqrt(square_mean - stash_mean * stash_mean + norm_epsilon)
    centred = (stashed - stash_mean) * inv_std
    grad_input = inv_std * (
        grad_scaled - grad_mean - centred * inv_std * (cross_mean - stash_mean * grad_mean)
    )
    grad_input = (upstream.astype(F32) + grad_input).astype(BF16)
    bwd_next = shifted(grad_input, "pipe", -1)

    fwd_next = s0.astype(F32) + s1.astype(F32) + s2.astype(F32) + s3.astype(F32)
    fwd_next = fwd_next.astype(BF16)
    return (fwd_next[None], bwd_next[None])


def solution(mesh):
    pipe = mesh.devices.shape[0]
    split = Mesh(mesh.devices.reshape(pipe, SIDE, SIDE), ("pipe", "y", "z"))
    tp = ("y", "z")
    placed = (
        P("pipe", None, tp),
        P("pipe", None, tp),
        P("pipe", tp),
        P("pipe", tp),
        P("pipe", None, tp),
        P("pipe", tp, None),
        P("pipe", tp, None, None),
        P("pipe", tp, None, None),
        P("pipe", None, tp),
        P("pipe", tp, None),
        P("pipe", None),
    )
    return jax.shard_map(
        per_device,
        mesh=split,
        in_specs=placed,
        out_specs=(P("pipe", None, tp), P("pipe", None, tp)),
        check_vma=False,
    )
```

```python
import jax
import jax.numpy as jnp
from jax import lax
from jax.experimental import pallas as pl
from jax.experimental.pallas import tpu as pltpu
from jax.sharding import Mesh, PartitionSpec as P

norm_epsilon = 1e-05
SIDE = 4
F32 = jnp.float32
BF16 = jnp.bfloat16
NT = (((1,), (1,)), ((), ()))
NN = (((1,), (0,)), ((), ()))
VMEM_LIMIT = 56 * 1024 * 1024


def turned(value, axis, steps):
    return lax.ppermute(value, axis, [(i, (i + steps) % SIDE) for i in range(SIDE)])


def shifted(value, axis, steps):
    count = lax.axis_size(axis)
    first, last = (max(0, -steps), min(count, count - steps))
    return lax.ppermute(value, axis, [(source, source + steps) for source in range(first, last)])


def shifted_turned(value, steps):
    count = lax.axis_size("pipe")
    pairs = [
        (s * SIDE + i, (s + 1) * SIDE + (i + steps) % SIDE)
        for s in range(count - 1)
        for i in range(SIDE)
    ]
    return lax.ppermute(value, ("pipe", "z"), pairs)


def mirrored(value):
    count = lax.axis_size("pipe")
    return lax.ppermute(value, "pipe", [(s, count - 1 - s) for s in range(count)])


def add(left, right):
    return (left.astype(F32) + right.astype(F32)).astype(BF16)


def weights_kernel(fwd_ref, bwd_ref, fwd_out, bwd_out):
    size = fwd_ref.shape[-1]
    query = lax.broadcasted_iota(jnp.int32, (size, size), 0)
    key = lax.broadcasted_iota(jnp.int32, (size, size), 1)

    def causal(scores):
        masked = jnp.where(key <= query, scores, -jnp.inf)
        raised = jnp.exp(masked - jnp.max(masked, axis=-1, keepdims=True))
        return raised / jnp.sum(raised, axis=-1, keepdims=True)

    for head in range(fwd_ref.shape[0]):
        bwd_out[head] = causal(bwd_ref[head]).T.astype(BF16)
        fwd_out[head] = causal(fwd_ref[head]).astype(BF16)


ORDER = [4, 5, 3, 6, 2, 7, 0, 1]


def start_weights(place, wv_hbm, wo_hbm, wv, wo, sem_v, sem_o, value_first):
    width = wv_hbm.shape[1]

    def copies(j, second):
        relative = second or (value_first and j // SIDE == 2)
        k = lax.rem(place[1] + j % SIDE, SIDE) if relative else j % SIDE
        block = lax.rem(place[0] + j // SIDE, SIDE) * SIDE + k
        at = pl.ds(pl.multiple_of(block * width, 128), width)
        here = slice(j * width, (j + 1) * width)
        if second != value_first:
            return pltpu.make_async_copy(wv_hbm.at[at, :], wv.at[here, :], sem_v.at[j])
        return pltpu.make_async_copy(wo_hbm.at[:, at], wo.at[:, here], sem_o.at[j])

    first = [copies(j, False) for j in range(SIDE * SIDE)]
    second = [copies(j, True) for j in range(SIDE * SIDE)]
    for c in first:
        c.start()
    for pair in ORDER:
        second[2 * pair].start()
        second[2 * pair + 1].start()
    return first, second


def start_pieces(refs, held, sem):
    near, right, left, far_a, far_b = refs
    two, three = pl.ds(0, 2), pl.ds(0, 3)
    if len(far_a.shape) == 2:
        far = [(far_a, held.at[8]), (far_b.at[three], held.at[pl.ds(9, 3)])]
    else:
        far = [(far_a.at[two], held.at[pl.ds(8, 2)]), (far_b.at[two], held.at[pl.ds(10, 2)])]
    moves = [
        (near, held.at[pl.ds(0, 4)]),
        (right, held.at[pl.ds(4, 4)]),
        *far,
        (left, held.at[pl.ds(12, 4)]),
    ]
    copies = [pltpu.make_async_copy(*move, sem.at[i]) for i, move in enumerate(moves)]
    for c in copies:
        c.start()
    return [copies[0:1], [], copies[1:2], [], copies[2:4], [], copies[4:5], []]


def give_parts(product, refs, parts, sem, width):
    p2a, p2b, p1, p3, p0 = refs
    outs = [(p0, 0), (p0, 2), (p1, 0), (p1, 2), (p2a, 0), (p2b, 0), (p3, 0), (p3, 2)]
    copies = []
    for pair in ORDER:
        ref, at = outs[pair]
        wide = product(pair).astype(BF16)
        parts[2 * pair] = wide[:, :width]
        parts[2 * pair + 1] = wide[:, width:]
        copies.append(
            pltpu.make_async_copy(
                parts.at[pl.ds(2 * pair, 2)], ref.at[pl.ds(at, 2)], sem.at[pair]
            )
        )
        copies[-1].start()
    for c in copies:
        c.wait()


def mix(weights, values):
    size = values.shape[1] // weights.shape[0]
    heads = [
        lax.dot_general(
            weights[h], values[:, h * size : (h + 1) * size], NN, preferred_element_type=F32
        ).astype(BF16)
        for h in range(weights.shape[0])
    ]
    return jnp.concatenate(heads, axis=1)


def bwd_kernel(
    place, near, right, left, fa, fb, weights, wv_hbm, wo_hbm,
    p2a, p2b, p1, p3, p0,
    held, parts, wv, wo, sem_in, sem_out, sem_v, sem_o,
):
    rows, width = parts.shape[1:]
    arriving = start_pieces((near, right, left, fa, fb), held, sem_in)
    out, value = start_weights(place, wv_hbm, wo_hbm, wv, wo, sem_v, sem_o, False)
    total = jnp.zeros((rows, width), F32)
    for pair in range(SIDE * SIDE // 2):
        for c in arriving[pair]:
            c.wait()
        out[2 * pair].wait()
        out[2 * pair + 1].wait()
        wide = jnp.concatenate([held[2 * pair], held[2 * pair + 1]], axis=1)
        total += lax.dot_general(
            wide, wo[:, 2 * pair * width : 2 * (pair + 1) * width], NT, preferred_element_type=F32
        )
    grads = mix(weights, total.astype(BF16))

    def product(pair):
        value[2 * pair].wait()
        value[2 * pair + 1].wait()
        return lax.dot_general(
            grads, wv[2 * pair * width : 2 * (pair + 1) * width, :], NT, preferred_element_type=F32
        )

    give_parts(product, (p2a, p2b, p1, p3, p0), parts, sem_out, width)


def fwd_kernel(
    place, near, right, left, fa, fb, weights, wv_hbm, wo_hbm,
    p2a, p2b, p1, p3, p0,
    held, parts, wv, wo, sem_in, sem_out, sem_v, sem_o,
):
    rows, width = parts.shape[1:]
    arriving = start_pieces((near, right, left, fa, fb), held, sem_in)
    value, out = start_weights(place, wv_hbm, wo_hbm, wv, wo, sem_v, sem_o, True)
    full = width * SIDE * SIDE
    sums = jnp.zeros((rows, 128), F32)
    squares = jnp.zeros((rows, 128), F32)
    for one in range(SIDE * SIDE):
        if one % 2 == 0:
            for c in arriving[one // 2]:
                c.wait()
        for c in range(0, width, 128):
            part = held[one, :rows, c : c + 128].astype(F32)
            sums += part
            squares += part * part
    mean = jnp.sum(sums, axis=-1, keepdims=True) / full
    var = jnp.sum(squares, axis=-1, keepdims=True) / full - mean * mean
    inv_std = lax.rsqrt(var + norm_epsilon)
    total = jnp.zeros((rows, width), F32)
    for pair in range(SIDE * SIDE // 2):
        value[2 * pair].wait()
        value[2 * pair + 1].wait()
        normed = []
        for one in (2 * pair, 2 * pair + 1):
            affine = held[one, rows : rows + 16, :].astype(F32)
            part = held[one, :rows, :].astype(F32)
            normed.append(((part - mean) * inv_std * affine[0:1] + affine[1:2]).astype(BF16))
        wide = jnp.concatenate(normed, axis=1)
        total += lax.dot_general(
            wide, wv[2 * pair * width : 2 * (pair + 1) * width, :], NN, preferred_element_type=F32
        )
    mixed = mix(weights, total.astype(BF16))

    def product(pair):
        out[2 * pair].wait()
        out[2 * pair + 1].wait()
        return lax.dot_general(
            mixed, wo[:, 2 * pair * width : 2 * (pair + 1) * width], NN, preferred_element_type=F32
        )

    give_parts(product, (p2a, p2b, p1, p3, p0), parts, sem_out, width)


def project(kernel, place, pieces, weights, w_value, w_out, rows):
    width = w_value.shape[1]
    half = jax.ShapeDtypeStruct((2, rows, width), BF16)
    whole = jax.ShapeDtypeStruct((4, rows, width), BF16)
    hbm = pl.BlockSpec(memory_space=pl.ANY)
    blocks = SIDE * SIDE
    flops = 4 * rows * width * width * blocks + 4 * rows * rows * width
    moved = 2 * 2 * width * width * blocks + 4 * rows * width * blocks
    return pl.pallas_call(
        kernel,
        out_shape=[half] * 2 + [whole] * 3,
        in_specs=[pl.BlockSpec(memory_space=pltpu.SMEM)]
        + [hbm] * 5
        + [pl.BlockSpec(memory_space=pltpu.VMEM)]
        + [hbm] * 2,
        out_specs=[hbm] * 5,
        scratch_shapes=[
            pltpu.VMEM((blocks, pieces[0].shape[1], width), BF16),
            pltpu.VMEM((blocks, rows, width), BF16),
            pltpu.VMEM((blocks * width, width), BF16),
            pltpu.VMEM((width, blocks * width), BF16),
            pltpu.SemaphoreType.DMA((blocks // 2,)),
            pltpu.SemaphoreType.DMA((blocks // 2,)),
            pltpu.SemaphoreType.DMA((blocks,)),
            pltpu.SemaphoreType.DMA((blocks,)),
        ],
        cost_estimate=pl.CostEstimate(flops=flops, bytes_accessed=moved, transcendentals=0),
        compiler_params=pltpu.CompilerParams(vmem_limit_bytes=VMEM_LIMIT),
    )(place, *pieces, weights, w_value, w_out)


def around(value):
    return turned(value, "z", -1), turned(value, "z", 2), turned(value, "z", 1)


def both_sides(value):
    return turned(value, "y", -1), turned(value, "y", 1)


def relayed(right, left):
    return turned(left[:2], "y", 1), turned(right[2:], "y", -1)


def joined(parts, by_left, by_right):
    _, _, p1, p3, p0 = parts
    p1 = jnp.concatenate([add(p1[:2], by_left), p1[2:]], axis=0)
    p3 = jnp.concatenate([p3[:2], add(p3[2:], by_right)], axis=0)
    return p1, p3, p0


def three(a, b, c):
    return (a.astype(F32) + b.astype(F32) + c.astype(F32)).astype(BF16)


def summed(value, axis):
    return value + turned(value, axis, 2) + turned(value, axis, 1) + turned(value, axis, -1)


def per_device(
    x_fwd,
    cotangent,
    ln_gain,
    ln_bias,
    w_value,
    w_out,
    scores_fwd,
    scores_bwd,
    stash_codes,
    stash_scales,
    evict,
):
    tokens, upstream = x_fwd[0], cotangent[0]
    rows, width = tokens.shape
    full = width * SIDE * SIDE
    value_proj, out_proj = w_value[0], w_out[0]
    place = jnp.stack([lax.axis_index("y"), lax.axis_index("z")]).astype(jnp.int32)

    ordered = lax.optimization_barrier
    affine = jnp.concatenate([ln_gain, ln_bias, jnp.zeros((14, width), BF16)], axis=0)
    tokens_affine = jnp.concatenate([tokens, affine], axis=0)
    near_up = lax.all_gather(upstream, "z", axis=0)
    right_up, left_up = both_sides(near_up)
    across = turned(tokens_affine, "y", 2)
    near_tok = lax.all_gather(tokens_affine, "z", axis=0)
    right_up, left_up, near_tok, across = ordered((right_up, left_up, near_tok, across))
    far_up = relayed(right_up, left_up)
    across_z = around(across)
    heads = scores_fwd.shape[1:]
    weights_fwd, weights_bwd = pl.pallas_call(
        weights_kernel,
        out_shape=[jax.ShapeDtypeStruct(heads, BF16)] * 2,
        compiler_params=pltpu.CompilerParams(vmem_limit_bytes=VMEM_LIMIT),
    )(scores_fwd[0], scores_bwd[0])

    far_up, near_tok, weights_bwd = ordered((far_up, near_tok, weights_bwd))
    right_tok, left_tok = both_sides(near_tok)

    projections = (value_proj, out_proj, rows)
    pieces_up = (near_up, right_up, left_up, *far_up)
    parts_bwd = project(bwd_kernel, place, pieces_up, weights_bwd, *projections)
    codes, scales = stash_codes[0], stash_scales[0]
    parts_bwd, across_z, codes, scales = ordered((parts_bwd, across_z, codes, scales))
    across_z = jnp.stack(across_z)
    blocks = scales.shape[0]
    scale_rows = blocks * rows // width
    fill = jnp.zeros((16 - scale_rows, width), BF16)
    stash = jnp.concatenate([codes, scales.reshape(scale_rows, width), fill])
    far_stash = mirrored(stash)
    passing_bwd = turned(parts_bwd[0], "y", 1), turned(parts_bwd[1], "y", -1)
    right_tok, left_tok, passing_bwd = ordered((right_tok, left_tok, passing_bwd))
    pieces_tok = (near_tok, right_tok, left_tok, across, across_z)
    p1, p3, p0 = joined(parts_bwd, *passing_bwd)
    by_left, by_right = turned(p1, "y", 1), turned(p3, "y", -1)
    parts_fwd = project(fwd_kernel, place, pieces_tok, weights_fwd, *projections)
    by_left, by_right, parts_fwd, far_stash = ordered((by_left, by_right, parts_fwd, far_stash))

    passing_fwd = turned(parts_fwd[0], "y", 1), turned(parts_fwd[1], "y", -1)
    by_left, by_right, passing_fwd = ordered((by_left, by_right, passing_fwd))
    q0, q1, q2, q3 = three(p0, by_left, by_right)
    r2, r1, r3 = turned(q2, "z", 2), turned(q1, "z", 1), turned(q3, "z", -1)
    p1, p3, p0 = joined(parts_fwd, *passing_fwd)
    by_left, by_right = turned(p1, "y", 1), turned(p3, "y", -1)
    by_left, by_right, r1, r2, r3 = ordered((by_left, by_right, r1, r2, r3))
    f0, f1, f2, f3 = three(p0, by_left, by_right)
    r1, r2, r3, f2 = ordered((r1, r2, r3, f2))
    f0 = add(f0, tokens)
    s2, s1 = shifted_turned(f2, 2), shifted_turned(f1, 1)
    s3, s0 = shifted_turned(f3, -1), shifted_turned(f0, 0)

    keep_own = evict[0] == lax.axis_index("pipe")
    far_scales = far_stash[rows : rows + scale_rows].reshape(blocks, rows)
    held_codes = jnp.where(keep_own[:, None], codes, far_stash[:rows])
    held_scales = jnp.where(keep_own[None, :], scales, far_scales)
    stashed = (
        held_codes.astype(F32).reshape(rows, blocks, width // blocks)
        * held_scales.astype(F32).T[:, :, None]
    ).reshape(rows, width)

    grad_normed = q0.astype(F32) + r1.astype(F32) + r2.astype(F32) + r3.astype(F32)
    grad_scaled = grad_normed * ln_gain[0].astype(F32)
    sums = jnp.stack(
        [
            jnp.sum(stashed, axis=-1),
            jnp.sum(stashed * stashed, axis=-1),
            jnp.sum(grad_scaled, axis=-1),
            jnp.sum(grad_scaled * stashed, axis=-1),
        ]
    )
    sums, s1, s2, s3 = ordered((summed(sums, "z"), s1, s2, s3))
    sums = summed(sums, "y") / full
    stash_mean, square_mean, grad_mean, cross_mean = (sums[i][:, None] for i in range(4))
    inv_std = lax.rsqrt(square_mean - stash_mean * stash_mean + norm_epsilon)
    centred = (stashed - stash_mean) * inv_std
    grad_input = inv_std * (
        grad_scaled - grad_mean - centred * inv_std * (cross_mean - stash_mean * grad_mean)
    )
    grad_input = (upstream.astype(F32) + grad_input).astype(BF16)
    bwd_next = shifted(grad_input, "pipe", -1)

    fwd_next = s0.astype(F32) + s1.astype(F32) + s2.astype(F32) + s3.astype(F32)
    fwd_next = fwd_next.astype(BF16)
    return (fwd_next[None], bwd_next[None])


def solution(mesh):
    pipe = mesh.devices.shape[0]
    split = Mesh(mesh.devices.reshape(pipe, SIDE, SIDE), ("pipe", "y", "z"))
    tp = ("y", "z")
    placed = (
        P("pipe", None, tp),
        P("pipe", None, tp),
        P("pipe", tp),
        P("pipe", tp),
        P("pipe", None, tp),
        P("pipe", tp, None),
        P("pipe", tp, None, None),
        P("pipe", tp, None, None),
        P("pipe", None, tp),
        P("pipe", tp, None),
        P("pipe", None),
    )
    return jax.shard_map(
        per_device,
        mesh=split,
        in_specs=placed,
        out_specs=(P("pipe", None, tp), P("pipe", None, tp)),
        check_vma=False,
    )
```
